32 devices in a mesh: groups: 2 (over x), aux: 16 (over z, y, core).
Axes of the slice: x: 2, y: 2, z: 4, core: 2. Of those that a mesh axis runs over, the one named last changes fastest.
Arguments:
- integrals: bfloat16 [1024, 3, 128, 3, 128], P(('groups', 'aux')), parts along dimension 0, may hold values from -0.3125 to 0.3125
- coeff: bfloat16 [8192, 1024], P(('groups', 'aux')), parts along dimension 0, may hold values from -0.046875 to 0.046875
- screen: int32 [32, 3], P(('groups', 'aux')), parts along dimension 0, may hold values from 0 to 5, as said below
- occ_ids: int32 [8], P('groups'), parts along dimension 0, may hold values from 0 to 7, as said below
Outputs:
- exchange_band: float32 [8192, 1280], P(('groups', 'aux')), parts along dimension 0
The draws below stay inside these ranges and needn't reach their ends.
There are 2 independent parts, one for each index of `groups`. The reference program is written for one: setup_inputs(seed, part) draws one part's arguments, and reference() takes and returns one part's arrays. A program takes and returns all parts, laid end to end along the dimension named above; each array names one. Nothing has to cross between parts.
Inputs may be any that keep to these rules, and one draw needn't show every extreme that they name: `screen`: each row holds 3 distinct positions, and 2 * row - 2 + value is always a basis block of the molecule. `occ_ids`: distinct occupied block ids.
All inputs are finite; a program needn't handle non-finite values.
Results may differ from the reference program's by a relative error of at most 0.00054.
Values may be sent and summed in bfloat16 or wider, within the bound.
A program may use at most 128 MiB of HBM per device.

```python
import jax
import jax.numpy as jnp
from jax import lax

AUX_DEV = 32
BLK = 128
BB_DEV = 2
NSB = 3
OCCB = 4
OCCA_B = 8
ABLK = 16
NAUX = 512
NBB = 32
NBAS = 4096
NOCC = 512
OCCALL = 1024


def draw_screen(key, part):
    key = jax.random.fold_in(key, 11)
    width = 3 * BB_DEV
    scores = jax.random.randint(key, (ABLK, width), 0, 1 << 20) * 8 + jnp.arange(width, dtype=jnp.int32)[None, :]
    rows = jnp.arange(ABLK, dtype=jnp.int32)[:, None]
    blocks = BB_DEV * rows - BB_DEV + jnp.arange(width, dtype=jnp.int32)[None, :]
    valid = (blocks >= 0) & (blocks < NBB)
    scores = jnp.where(valid, scores, -1)
    return jax.lax.top_k(scores, NSB)[1].astype(jnp.int32)


def draw_occ_ids(key, part):
    key = jax.random.fold_in(key, 12)
    first_key, second_key = jax.random.split(key)
    middle = (jax.random.permutation(first_key, OCCA_B - 2)[:OCCB - 2] + 1).astype(jnp.int32)
    chosen = jnp.concatenate([jnp.array([0, OCCA_B - 1], dtype=jnp.int32), middle])
    return jax.random.permutation(second_key, chosen).astype(jnp.int32)


def levels(own_key, shape, cuts, smallest, high):
    level, own = 1.0, jax.random.fold_in(own_key, 6)
    for dim, parts in cuts:
        heights = jnp.exp(jax.random.uniform(jax.random.fold_in(own, dim), (parts,), jnp.float32, smallest / len(cuts), high / len(cuts)))
        level = level * jnp.repeat(heights, shape[dim] // parts).reshape([-1 if axis == dim else 1 for axis in range(len(shape))])
    return level


def bell_draw(key, dims, spread, bound, cuts=(), kind=jnp.bfloat16):
    loudness = levels(key, dims, cuts, -0.22, 0.18) if cuts else 1.0
    entries = jax.random.normal(key, dims, jnp.float32) * spread * loudness
    return jnp.minimum(jnp.maximum(entries, -bound), bound).astype(kind)


def setup_inputs(seed: int = 0, part: int = 0) -> dict:
    arg_keys = jax.random.split(jax.random.key(seed), 5)
    part_splits = jax.random.split(jax.random.fold_in(arg_keys[4], part), 5)
    integrals = bell_draw(part_splits[0], (NAUX, NSB, BLK, NSB, BLK), (NSB * BLK) ** -0.5, 0.3125, ((0, 16),))
    coeff = bell_draw(part_splits[1], (NBAS, OCCALL), (AUX_DEV * OCCB * BLK) ** -0.5, 0.046875, ((0, 16),))
    screen = draw_screen(jax.random.fold_in(jax.random.fold_in(arg_keys[4], part), 71), part)
    occ_ids = draw_occ_ids(jax.random.fold_in(jax.random.fold_in(arg_keys[4], part), 71), part)
    return {"integrals": integrals, "coeff": coeff, "screen": screen, "occ_ids": occ_ids}


def reference(integrals, coeff, screen, occ_ids):
    occupied = jnp.take(coeff.reshape(NBAS, OCCA_B, BLK), occ_ids, axis=1).reshape(NBAS, NOCC)
    blocks = occupied.reshape(NBB, BLK, NOCC)
    band = jnp.zeros((NBAS, 5 * BB_DEV * BLK), jnp.float32)

    def one_block(index, band):
        index = jnp.asarray(index).astype(jnp.int32)
        local = lax.dynamic_slice_in_dim(integrals, index * AUX_DEV, AUX_DEV, 0)
        ids = lax.dynamic_slice_in_dim(screen, index, 1, 0)[0].astype(jnp.int32)
        global_ids = (BB_DEV * index - BB_DEV + ids).astype(jnp.int32)
        picked = jnp.take(blocks, global_ids, axis=0)
        half = jnp.dot(local.reshape(AUX_DEV * NSB * BLK, NSB * BLK), picked.reshape(NSB * BLK, NOCC), preferred_element_type=jnp.float32)
        half = half.astype(jnp.bfloat16).reshape(AUX_DEV, NSB * BLK, NOCC)
        partial_value = lax.dot_general(half, half, (((0, 2), (0, 2)), ((), ())), preferred_element_type=jnp.float32)
        partial_value = partial_value.reshape(NSB, BLK, NSB, BLK)
        for first in range(NSB):
            row_block = global_ids[first]
            base = BB_DEV * (row_block // BB_DEV) - 2 * BB_DEV
            for second in range(NSB):
                column = (global_ids[second] - base).astype(jnp.int32)
                start_row = (row_block * BLK).astype(jnp.int32)
                start_col = (column * BLK).astype(jnp.int32)
                current = lax.dynamic_slice(band, (start_row, start_col), (BLK, BLK))
                band = lax.dynamic_update_slice(band, current + partial_value[first, :, second, :], (start_row, start_col))
        return band

    return lax.fori_loop(0, ABLK, one_block, band)
```

```python
import jax
import jax.numpy as jnp
from jax import lax
from jax.experimental import pallas as pl
from jax.experimental.pallas import tpu as pltpu
from jax.sharding import PartitionSpec as P

BLK = 128
BB_DEV = 2
NSB = 3
OCCB = 4
OCCA_B = 8
EDGE = BB_DEV * BLK
STEP = 2
MIB = 1 << 20


def kernel(count, ints, coeff, screen, occ_ids, band, buf, window, picked, total, ext, out_prev, out_next,
           in_prev, in_next, ids_prev, ids_next, load_sem, occ_send, occ_recv, id_send, id_recv, row_send, row_recv):
    me = lax.axis_index("aux")
    has_prev, has_next = me > 0, me < count - 1
    aux_rows = ints.shape[0]
    steps = aux_rows // STEP

    barrier = pltpu.get_barrier_semaphore()

    @pl.when(has_prev)
    def _():
        pl.semaphore_signal(barrier, inc=1, device_id={"aux": me - 1}, device_id_type=pl.DeviceIdType.MESH)

    @pl.when(has_next)
    def _():
        pl.semaphore_signal(barrier, inc=1, device_id={"aux": me + 1}, device_id_type=pl.DeviceIdType.MESH)

    def load(step):
        part = pl.ds(step * STEP, STEP)
        return pltpu.make_async_copy(ints.at[part], buf.at[part], load_sem.at[step])

    @pl.loop(0, steps)
    def _(step):
        load(step).start()

    def pick(index, blocks):
        return sum(block * (index == k).astype(jnp.float32).astype(block.dtype) for k, block in enumerate(blocks))

    for o in range(OCCB):
        chosen = pick(occ_ids[o], [coeff[:, k * BLK : (k + 1) * BLK] for k in range(OCCA_B)])
        for r in range(BB_DEV):
            window[BB_DEV + r, :, o * BLK : (o + 1) * BLK] = chosen[r * BLK : (r + 1) * BLK]

    def remote(src, dst, send, recv, device):
        return pltpu.make_async_remote_copy(
            src_ref=src, dst_ref=dst, send_sem=send, recv_sem=recv,
            device_id={"aux": device}, device_id_type=pl.DeviceIdType.MESH)

    own = window.at[BB_DEV : 2 * BB_DEV]
    occ_down = remote(own, window.at[2 * BB_DEV : 3 * BB_DEV], occ_send.at[0], occ_recv.at[0], me - 1)
    occ_up = remote(own, window.at[0:BB_DEV], occ_send.at[1], occ_recv.at[1], me + 1)
    id_down = remote(screen, ids_next, id_send.at[0], id_recv.at[0], me - 1)
    id_up = remote(screen, ids_prev, id_send.at[1], id_recv.at[1], me + 1)

    pl.semaphore_wait(barrier, has_prev.astype(jnp.int32) + has_next.astype(jnp.int32))

    @pl.when(has_prev)
    def _():
        occ_down.start()
        id_down.start()

    @pl.when(has_next)
    def _():
        occ_up.start()
        id_up.start()

    total[...] = jnp.zeros_like(total)
    zero = jnp.zeros((BLK, BLK), jnp.float32)
    @pl.when(has_next)
    def _():
        occ_down.wait_recv()

    @pl.when(jnp.logical_not(has_next))
    def _():
        window[2 * BB_DEV : 3 * BB_DEV] = jnp.zeros((BB_DEV, BLK, OCCB * BLK), window.dtype)

    @pl.when(has_prev)
    def _():
        occ_up.wait_recv()

    @pl.when(jnp.logical_not(has_prev))
    def _():
        window[0:BB_DEV] = jnp.zeros((BB_DEV, BLK, OCCB * BLK), window.dtype)

    for t in range(NSB):
        picked[t * BLK : (t + 1) * BLK] = pick(screen[0, t], [window[w] for w in range(3 * BB_DEV)])

    nt = (((1,), (1,)), ((), ()))

    @pl.loop(0, steps)
    def _(step):
        load(step).wait()
        halves = []
        for p in range(STEP):
            x = buf[step * STEP + p]
            left = jnp.concatenate([x[:, t].reshape(NSB * BLK, BLK) for t in range(NSB)], axis=1)
            halves.append(jnp.dot(left, picked[...], preferred_element_type=jnp.float32).astype(jnp.bfloat16))
        half = jnp.concatenate(halves, axis=1)
        low = half[: 2 * BLK]
        high = half[2 * BLK :]
        total[:, : 2 * BLK] += lax.dot_general(half, low, nt, preferred_element_type=jnp.float32)
        total[2 * BLK :, 2 * BLK :] += lax.dot_general(high, high, nt, preferred_element_type=jnp.float32)

    for s in range(NSB):
        for t in range(NSB):
            if t == 2 and s < 2:
                block = total[2 * BLK :, s * BLK : (s + 1) * BLK].T
            else:
                block = total[s * BLK : (s + 1) * BLK, t * BLK : (t + 1) * BLK]
            ext[s * NSB + t] = block

    def put(ids, w, blocks):
        return sum(block * (ids[0, t] == w).astype(jnp.float32) for t, block in enumerate(blocks))

    def row(w):
        return [put(screen, w, [ext[s * NSB + t] for s in range(NSB)]) for t in range(NSB)]

    def rows(side, w):
        for t, block in enumerate(row(w)):
            side[w % BB_DEV, t] = block

    downs, ups = [], []
    for r in range(BB_DEV):
        downs.append(remote(out_prev.at[r], in_next.at[r], row_send.at[r], row_recv.at[r], me - 1))
        ups.append(remote(out_next.at[r], in_prev.at[r], row_send.at[2 + r], row_recv.at[2 + r], me + 1))
    for r in range(BB_DEV):
        rows(out_prev, r)

        @pl.when(has_prev)
        def _():
            downs[r].start()

        rows(out_next, 2 * BB_DEV + r)

        @pl.when(has_next)
        def _():
            ups[r].start()

    def place(r, j):
        return slice(r * BLK, (r + 1) * BLK), slice(j * BLK, (j + 1) * BLK)

    for r in range(BB_DEV):
        own_row = row(BB_DEV + r)
        for j in range(5 * BB_DEV):
            if BB_DEV <= j < 4 * BB_DEV:
                band[place(r, j)] = put(screen, j - BB_DEV, own_row)
            else:
                band[place(r, j)] = zero

    @pl.when(has_prev)
    def _():
        occ_down.wait_send()
        id_down.wait_send()
        id_up.wait_recv()
        for r in range(BB_DEV):
            ups[r].wait_recv()
        for r in range(BB_DEV):
            for j in range(3 * BB_DEV):
                band[place(r, j)] += put(ids_prev, j, [in_prev[r, t] for t in range(NSB)])

    @pl.when(has_next)
    def _():
        occ_up.wait_send()
        id_up.wait_send()
        id_down.wait_recv()
        for r in range(BB_DEV):
            downs[r].wait_recv()
        for r in range(BB_DEV):
            for j in range(3 * BB_DEV):
                band[place(r, j + 2 * BB_DEV)] += put(ids_next, j, [in_next[r, t] for t in range(NSB)])

    @pl.when(has_prev)
    def _():
        for r in range(BB_DEV):
            downs[r].wait_send()

    @pl.when(has_next)
    def _():
        for r in range(BB_DEV):
            ups[r].wait_send()


def solution(mesh):
    count = mesh.shape["aux"]

    def shards(integrals, coeff, screen, occ_ids):
        aux_rows = integrals.shape[0]
        ints = jnp.transpose(integrals, (0, 1, 3, 2, 4))
        vmem = pl.BlockSpec(memory_space=pltpu.VMEM)
        smem = pl.BlockSpec(memory_space=pltpu.SMEM)
        nocc = OCCB * BLK
        dma = pltpu.SemaphoreType.DMA
        return pl.pallas_call(
            lambda *refs: kernel(count, *refs),
            out_shape=jax.ShapeDtypeStruct((EDGE, 5 * EDGE), jnp.float32),
            in_specs=[pl.BlockSpec(memory_space=pl.ANY), vmem, smem, smem],
            out_specs=vmem,
            scratch_shapes=[
                pltpu.VMEM((aux_rows, NSB, NSB, BLK, BLK), jnp.bfloat16),
                pltpu.VMEM((3 * BB_DEV, BLK, nocc), jnp.bfloat16),
                pltpu.VMEM((NSB * BLK, nocc), jnp.bfloat16),
                pltpu.VMEM((NSB * BLK, NSB * BLK), jnp.float32),
                pltpu.VMEM((NSB * NSB, BLK, BLK), jnp.float32),
                pltpu.VMEM((BB_DEV, NSB, BLK, BLK), jnp.float32),
                pltpu.VMEM((BB_DEV, NSB, BLK, BLK), jnp.float32),
                pltpu.VMEM((BB_DEV, NSB, BLK, BLK), jnp.float32),
                pltpu.VMEM((BB_DEV, NSB, BLK, BLK), jnp.float32),
                pltpu.SMEM((1, NSB), jnp.int32),
                pltpu.SMEM((1, NSB), jnp.int32),
                dma((aux_rows // STEP,)),
                dma((2,)),
                dma((2,)),
                dma((2,)),
                dma((2,)),
                dma((4,)),
                dma((4,)),
            ],
            compiler_params=pltpu.CompilerParams(
                collective_id=0, has_side_effects=True, vmem_limit_bytes=40 * MIB),
            cost_estimate=pl.CostEstimate(
                flops=4 * aux_rows * NSB * BLK * NSB * BLK * nocc, transcendentals=0,
                bytes_accessed=aux_rows * (NSB * BLK) ** 2 * 2),
        )(ints, coeff, screen, occ_ids)

    return jax.shard_map(
        shards,
        mesh=mesh,
        in_specs=(
            P(("groups", "aux"), None, None, None, None),
            P(("groups", "aux"), None),
            P(("groups", "aux"), None),
            P("groups"),
        ),
        out_specs=P(("groups", "aux"), None),
        check_vma=False,
    )
```

```python
import jax
import jax.numpy as jnp
from jax import lax
from jax.experimental import pallas as pl
from jax.experimental.pallas import tpu as pltpu
from jax.sharding import PartitionSpec as P

BLK = 128
BB_DEV = 2
NSB = 3
OCCB = 4
OCCA_B = 8
EDGE = BB_DEV * BLK
STEP = 8
CUTS = 2
PART = OCCB // CUTS
MIB = 1 << 20
TOP = 46340.0


def kernel(count, ints, coeff_hbm, screen_hbm, occ_hbm, band, coeff, screen, occ_ids, buf, window, picked, total, ext, out_prev, out_next,
           in_prev, in_next, ids_prev, ids_next, load_sem, occ_send, occ_recv, id_send, id_recv, row_send, row_recv, arg_sem,
           unit_out, unit_prev, unit_next, unit_send, unit_recv):
    me = lax.axis_index("aux")
    has_prev, has_next = me > 0, me < count - 1
    aux_rows = ints.shape[0]
    steps = aux_rows // STEP

    fetches = [
        pltpu.make_async_copy(src, dst, arg_sem.at[i])
        for i, (src, dst) in enumerate([(occ_hbm, occ_ids), (coeff_hbm, coeff), (screen_hbm, screen)])
    ]
    for fetch in fetches:
        fetch.start()

    barrier = pltpu.get_barrier_semaphore()

    @pl.when(has_prev)
    def _():
        pl.semaphore_signal(barrier, inc=1, device_id={"aux": me - 1}, device_id_type=pl.DeviceIdType.MESH)

    @pl.when(has_next)
    def _():
        pl.semaphore_signal(barrier, inc=1, device_id={"aux": me + 1}, device_id_type=pl.DeviceIdType.MESH)

    def load(step):
        part = pl.ds(step * STEP, STEP)
        return pltpu.make_async_copy(ints.at[part], buf.at[part], load_sem.at[step])

    @pl.loop(0, steps)
    def _(step):
        load(step).start()

    for fetch in fetches:
        fetch.wait()

    def pick(index, blocks):
        return sum(block * (index == k).astype(jnp.float32).astype(block.dtype) for k, block in enumerate(blocks))

    def remote(src, dst, send, recv, device):
        return pltpu.make_async_remote_copy(
            src_ref=src, dst_ref=dst, send_sem=send, recv_sem=recv,
            device_id={"aux": device}, device_id_type=pl.DeviceIdType.MESH)

    occ_down, occ_up = [], []
    for cut in range(CUTS):
        own = window.at[cut, BB_DEV : 2 * BB_DEV]
        occ_down.append(remote(own, window.at[cut, 2 * BB_DEV : 3 * BB_DEV], occ_send.at[cut], occ_recv.at[cut], me - 1))
        occ_up.append(remote(own, window.at[cut, 0:BB_DEV], occ_send.at[CUTS + cut], occ_recv.at[CUTS + cut], me + 1))
    id_down = remote(screen, ids_next, id_send.at[0], id_recv.at[0], me - 1)
    id_up = remote(screen, ids_prev, id_send.at[1], id_recv.at[1], me + 1)

    for cut in range(CUTS):
        for c in range(PART):
            chosen = pick(occ_ids[cut * PART + c], [coeff[:, k * BLK : (k + 1) * BLK] for k in range(OCCA_B)])
            for r in range(BB_DEV):
                window[cut, BB_DEV + r, :, c * BLK : (c + 1) * BLK] = chosen[r * BLK : (r + 1) * BLK]
        if cut == 0:
            pl.semaphore_wait(barrier, has_prev.astype(jnp.int32) + has_next.astype(jnp.int32))

        @pl.when(has_prev)
        def _():
            occ_down[cut].start()
            if cut == CUTS - 1:
                id_down.start()

        @pl.when(has_next)
        def _():
            occ_up[cut].start()
            if cut == CUTS - 1:
                id_up.start()

    total[...] = jnp.zeros_like(total)
    zero = jnp.zeros((BLK, BLK), jnp.float32)
    blank = jnp.zeros((BB_DEV, BLK, PART * BLK), window.dtype)
    nt = (((1,), (1,)), ((), ()))
    for cut in range(CUTS):

        @pl.when(has_next)
        def _():
            occ_down[cut].wait_recv()

        @pl.when(jnp.logical_not(has_next))
        def _():
            window[cut, 2 * BB_DEV : 3 * BB_DEV] = blank

        @pl.when(has_prev)
        def _():
            occ_up[cut].wait_recv()

        @pl.when(jnp.logical_not(has_prev))
        def _():
            window[cut, 0:BB_DEV] = blank

        for t in range(NSB):
            picked[cut, t * BLK : (t + 1) * BLK] = pick(screen[0, t], [window[cut, w] for w in range(3 * BB_DEV)])

        @pl.loop(0, steps)
        def _(step):
            if cut == 0:
                load(step).wait()
            halves = []
            for p in range(STEP):
                x = buf[step * STEP + p]
                left = jnp.concatenate([x[:, t].reshape(NSB * BLK, BLK) for t in range(NSB)], axis=1)
                halves.append(jnp.dot(left, picked[cut], preferred_element_type=jnp.float32).astype(jnp.bfloat16))
            half = jnp.concatenate(halves, axis=1)
            low = half[: 2 * BLK]
            high = half[2 * BLK :]
            total[:, : 2 * BLK] += lax.dot_general(half, low, nt, preferred_element_type=jnp.float32)
            total[2 * BLK :, 2 * BLK :] += lax.dot_general(high, high, nt, preferred_element_type=jnp.float32)

    for s in range(NSB):
        for t in range(NSB):
            if t == 2 and s < 2:
                block = total[2 * BLK :, s * BLK : (s + 1) * BLK].T
            else:
                block = total[s * BLK : (s + 1) * BLK, t * BLK : (t + 1) * BLK]
            ext[s * NSB + t] = block

    def put(ids, w, blocks):
        return sum(block * (ids[0, t] == w).astype(jnp.float32) for t, block in enumerate(blocks))

    def row(w):
        return [put(screen, w, [ext[s * NSB + t] for s in range(NSB)]) for t in range(NSB)]

    def rows(side, w):
        for t, block in enumerate(row(w)):
            side[w % BB_DEV, t] = code(block)

    largest = jnp.maximum(ext[0], jnp.maximum(ext[NSB + 1], ext[2 * NSB + 2]))
    largest = jnp.maximum(jnp.max(largest, axis=(0, 1), keepdims=True), 1e-30)
    unit_out[...] = jnp.broadcast_to(largest * (1.0 / TOP), unit_out.shape)
    grow = TOP / largest

    def code(block):
        x = block * grow
        x2 = x * x
        return ((x2 * x2) * (x2 * (x * jnp.abs(x)))).astype(jnp.bfloat16)

    def decode(block, unit):
        y = block.astype(jnp.float32)
        root = lax.rsqrt(lax.rsqrt(jnp.maximum(jnp.abs(y), 1e-37)))
        root = root * lax.rsqrt(root) * unit[0:1]
        return jnp.where(y < 0, -root, jnp.where(y > 0, root, 0.0))

    unit_down = remote(unit_out, unit_next, unit_send.at[0], unit_recv.at[0], me - 1)
    unit_up = remote(unit_out, unit_prev, unit_send.at[1], unit_recv.at[1], me + 1)

    @pl.when(has_prev)
    def _():
        unit_down.start()

    @pl.when(has_next)
    def _():
        unit_up.start()

    downs, ups = [], []
    for r in range(BB_DEV):
        downs.append(remote(out_prev.at[r], in_next.at[r], row_send.at[r], row_recv.at[r], me - 1))
        ups.append(remote(out_next.at[r], in_prev.at[r], row_send.at[2 + r], row_recv.at[2 + r], me + 1))
    for r in range(BB_DEV):
        rows(out_prev, r)

        @pl.when(has_prev)
        def _():
            downs[r].start()

        rows(out_next, 2 * BB_DEV + r)

        @pl.when(has_next)
        def _():
            ups[r].start()

    def place(r, j):
        return slice(r * BLK, (r + 1) * BLK), slice(j * BLK, (j + 1) * BLK)

    for r in range(BB_DEV):
        own_row = row(BB_DEV + r)
        for j in range(5 * BB_DEV):
            if BB_DEV <= j < 4 * BB_DEV:
                band[place(r, j)] = put(screen, j - BB_DEV, own_row)
            else:
                band[place(r, j)] = zero

    @pl.when(has_prev)
    def _():
        for cut in range(CUTS):
            occ_down[cut].wait_send()
        id_down.wait_send()
        id_up.wait_recv()
        unit_down.wait_send()
        unit_up.wait_recv()
        for r in range(BB_DEV):
            ups[r].wait_recv()
        for r in range(BB_DEV):
            came = [decode(in_prev[r, t], unit_prev) for t in range(NSB)]
            for j in range(3 * BB_DEV):
                band[place(r, j)] += put(ids_prev, j, came)

    @pl.when(has_next)
    def _():
        for cut in range(CUTS):
            occ_up[cut].wait_send()
        id_up.wait_send()
        id_down.wait_recv()
        unit_up.wait_send()
        unit_down.wait_recv()
        for r in range(BB_DEV):
            downs[r].wait_recv()
        for r in range(BB_DEV):
            came = [decode(in_next[r, t], unit_next) for t in range(NSB)]
            for j in range(3 * BB_DEV):
                band[place(r, j + 2 * BB_DEV)] += put(ids_next, j, came)

    @pl.when(has_prev)
    def _():
        for r in range(BB_DEV):
            downs[r].wait_send()

    @pl.when(has_next)
    def _():
        for r in range(BB_DEV):
            ups[r].wait_send()


def solution(mesh):
    count = mesh.shape["aux"]

    def shards(integrals, coeff, screen, occ_ids):
        aux_rows = integrals.shape[0]
        ints = jnp.transpose(integrals, (0, 1, 3, 2, 4))
        vmem = pl.BlockSpec(memory_space=pltpu.VMEM)
        nocc = OCCB * BLK
        dma = pltpu.SemaphoreType.DMA
        return pl.pallas_call(
            lambda *refs: kernel(count, *refs),
            out_shape=jax.ShapeDtypeStruct((EDGE, 5 * EDGE), jnp.float32),
            in_specs=[pl.BlockSpec(memory_space=pltpu.HBM)] * 4,
            out_specs=vmem,
            scratch_shapes=[
                pltpu.VMEM(coeff.shape, coeff.dtype),
                pltpu.SMEM(screen.shape, screen.dtype),
                pltpu.SMEM(occ_ids.shape, occ_ids.dtype),
                pltpu.VMEM((aux_rows, NSB, NSB, BLK, BLK), jnp.bfloat16),
                pltpu.VMEM((CUTS, 3 * BB_DEV, BLK, PART * BLK), jnp.bfloat16),
                pltpu.VMEM((CUTS, NSB * BLK, PART * BLK), jnp.bfloat16),
                pltpu.VMEM((NSB * BLK, NSB * BLK), jnp.float32),
                pltpu.VMEM((NSB * NSB, BLK, BLK), jnp.float32),
                pltpu.VMEM((BB_DEV, NSB, BLK, BLK), jnp.bfloat16),
                pltpu.VMEM((BB_DEV, NSB, BLK, BLK), jnp.bfloat16),
                pltpu.VMEM((BB_DEV, NSB, BLK, BLK), jnp.bfloat16),
                pltpu.VMEM((BB_DEV, NSB, BLK, BLK), jnp.bfloat16),
                pltpu.SMEM((1, NSB), jnp.int32),
                pltpu.SMEM((1, NSB), jnp.int32),
                dma((aux_rows // STEP,)),
                dma((2 * CUTS,)),
                dma((2 * CUTS,)),
                dma((2,)),
                dma((2,)),
                dma((4,)),
                dma((4,)),
                dma((3,)),
                pltpu.VMEM((8, BLK), jnp.float32),
                pltpu.VMEM((8, BLK), jnp.float32),
                pltpu.VMEM((8, BLK), jnp.float32),
                dma((2,)),
                dma((2,)),
            ],
            compiler_params=pltpu.CompilerParams(
                collective_id=0, has_side_effects=True, vmem_limit_bytes=56 * MIB),
            cost_estimate=pl.CostEstimate(
                flops=4 * aux_rows * NSB * BLK * NSB * BLK * nocc, transcendentals=0,
                bytes_accessed=aux_rows * (NSB * BLK) ** 2 * 2),
        )(ints, coeff, screen, occ_ids)

    return jax.shard_map(
        shards,
        mesh=mesh,
        in_specs=(
            P(("groups", "aux"), None, None, None, None),
            P(("groups", "aux"), None),
            P(("groups", "aux"), None),
            P("groups"),
        ),
        out_specs=P(("groups", "aux"), None),
        check_vma=False,
    )
```

```python
import jax
import jax.numpy as jnp
from jax import lax
from jax.experimental import pallas as pl
from jax.experimental.pallas import tpu as pltpu
from jax.sharding import PartitionSpec as P

BLK = 128
BB_DEV = 2
NSB = 3
OCCB = 4
OCCA_B = 8
EDGE = BB_DEV * BLK
STEP = 8
CUTS = 2
PART = OCCB // CUTS
MIB = 1 << 20
TOP = 46340.0


def kernel(count, ints, coeff_hbm, screen_hbm, occ_hbm, band, coeff, screen, occ_ids, buf, window, picked, total, ext, out_prev, out_next,
           in_prev, in_next, ids_prev, ids_next, load_sem, occ_send, occ_recv, id_send, id_recv, row_send, row_recv, arg_sem,
           unit_out, unit_prev, unit_next, unit_send, unit_recv):
    me = lax.axis_index("aux")
    has_prev, has_next = me > 0, me < count - 1
    aux_rows = ints.shape[0]
    steps = aux_rows // STEP

    fetches = [
        pltpu.make_async_copy(src, dst, arg_sem.at[i])
        for i, (src, dst) in enumerate([(occ_hbm, occ_ids), (coeff_hbm, coeff), (screen_hbm, screen)])
    ]
    for fetch in fetches:
        fetch.start()

    barrier = pltpu.get_barrier_semaphore()

    @pl.when(has_prev)
    def _():
        pl.semaphore_signal(barrier, inc=1, device_id={"aux": me - 1}, device_id_type=pl.DeviceIdType.MESH)

    @pl.when(has_next)
    def _():
        pl.semaphore_signal(barrier, inc=1, device_id={"aux": me + 1}, device_id_type=pl.DeviceIdType.MESH)

    def load(step):
        part = pl.ds(step * STEP, STEP)
        return pltpu.make_async_copy(ints.at[part], buf.at[part], load_sem.at[step])

    @pl.loop(0, steps)
    def _(step):
        load(step).start()

    for fetch in fetches:
        fetch.wait()

    def pick(index, blocks):
        return sum(block * (index == k).astype(jnp.float32).astype(block.dtype) for k, block in enumerate(blocks))

    def remote(src, dst, send, recv, device):
        return pltpu.make_async_remote_copy(
            src_ref=src, dst_ref=dst, send_sem=send, recv_sem=recv,
            device_id={"aux": device}, device_id_type=pl.DeviceIdType.MESH)

    occ_down, occ_up = [], []
    for cut in range(CUTS):
        own = window.at[cut, BB_DEV : 2 * BB_DEV]
        occ_down.append(remote(own, window.at[cut, 2 * BB_DEV : 3 * BB_DEV], occ_send.at[cut], occ_recv.at[cut], me - 1))
        occ_up.append(remote(own, window.at[cut, 0:BB_DEV], occ_send.at[CUTS + cut], occ_recv.at[CUTS + cut], me + 1))
    id_down = remote(screen, ids_next, id_send.at[0], id_recv.at[0], me - 1)
    id_up = remote(screen, ids_prev, id_send.at[1], id_recv.at[1], me + 1)

    for cut in range(CUTS):
        for c in range(PART):
            chosen = pick(occ_ids[cut * PART + c], [coeff[:, k * BLK : (k + 1) * BLK] for k in range(OCCA_B)])
            for r in range(BB_DEV):
                window[cut, BB_DEV + r, :, c * BLK : (c + 1) * BLK] = chosen[r * BLK : (r + 1) * BLK]
        if cut == 0:
            pl.semaphore_wait(barrier, has_prev.astype(jnp.int32) + has_next.astype(jnp.int32))

        @pl.when(has_prev)
        def _():
            occ_down[cut].start()
            if cut == CUTS - 1:
                id_down.start()

        @pl.when(has_next)
        def _():
            occ_up[cut].start()
            if cut == CUTS - 1:
                id_up.start()

    total[...] = jnp.zeros_like(total)
    zero = jnp.zeros((BLK, BLK), jnp.float32)
    blank = jnp.zeros((BB_DEV, BLK, PART * BLK), window.dtype)
    nt = (((1,), (1,)), ((), ()))
    for cut in range(CUTS):

        @pl.when(has_next)
        def _():
            occ_down[cut].wait_recv()

        @pl.when(jnp.logical_not(has_next))
        def _():
            window[cut, 2 * BB_DEV : 3 * BB_DEV] = blank

        @pl.when(has_prev)
        def _():
            occ_up[cut].wait_recv()

        @pl.when(jnp.logical_not(has_prev))
        def _():
            window[cut, 0:BB_DEV] = blank

        for t in range(NSB):
            picked[cut, t * BLK : (t + 1) * BLK] = pick(screen[0, t], [window[cut, w] for w in range(3 * BB_DEV)])

        @pl.loop(0, steps)
        def _(step):
            if cut == 0:
                load(step).wait()
            halves = []
            for p in range(STEP):
                x = buf[step * STEP + p]
                left = jnp.concatenate([x[:, t].reshape(NSB * BLK, BLK) for t in range(NSB)], axis=1)
                halves.append(jnp.dot(left, picked[cut], preferred_element_type=jnp.float32).astype(jnp.bfloat16))
            half = jnp.concatenate(halves, axis=1)
            low = half[: 2 * BLK]
            high = half[2 * BLK :]
            total[:, : 2 * BLK] += lax.dot_general(half, low, nt, preferred_element_type=jnp.float32)
            total[2 * BLK :, 2 * BLK :] += lax.dot_general(high, high, nt, preferred_element_type=jnp.float32)

    for s in range(NSB):
        for t in range(NSB):
            if t == 2 and s < 2:
                block = total[2 * BLK :, s * BLK : (s + 1) * BLK].T
            else:
                block = total[s * BLK : (s + 1) * BLK, t * BLK : (t + 1) * BLK]
            ext[s * NSB + t] = block

    def put(ids, w, blocks):
        return sum(block * (ids[0, t] == w).astype(jnp.float32) for t, block in enumerate(blocks))

    def row(w):
        return [put(screen, w, [ext[s * NSB + t] for s in range(NSB)]) for t in range(NSB)]

    def rows(side, w):
        for t, block in enumerate(row(w)):
            side[w % BB_DEV, t] = code(block)

    largest = jnp.maximum(ext[0], jnp.maximum(ext[NSB + 1], ext[2 * NSB + 2]))
    largest = jnp.maximum(jnp.max(largest, axis=(0, 1), keepdims=True), 1e-30)
    unit_out[...] = jnp.broadcast_to(largest * (1.0 / TOP), unit_out.shape)
    grow = TOP / largest

    def code(block):
        x = block * grow
        x2 = x * x
        return ((x2 * x2) * (x2 * (x * jnp.abs(x)))).astype(jnp.bfloat16)

    def decode(block, unit):
        y = block.astype(jnp.float32)
        root = lax.rsqrt(lax.rsqrt(jnp.maximum(jnp.abs(y), 1e-37)))
        root = root * lax.rsqrt(root) * unit[0:1]
        return jnp.where(y < 0, -root, jnp.where(y > 0, root, 0.0))

    unit_down = remote(unit_out, unit_next, unit_send.at[0], unit_recv.at[0], me - 1)
    unit_up = remote(unit_out, unit_prev, unit_send.at[1], unit_recv.at[1], me + 1)

    @pl.when(has_prev)
    def _():
        unit_down.start()

    @pl.when(has_next)
    def _():
        unit_up.start()

    downs, ups = [], []
    for r in range(BB_DEV):
        downs.append(remote(out_prev.at[r], in_next.at[r], row_send.at[r], row_recv.at[r], me - 1))
        ups.append(remote(out_next.at[r], in_prev.at[r], row_send.at[2 + r], row_recv.at[2 + r], me + 1))
    for r in range(BB_DEV):
        rows(out_prev, r)

        @pl.when(has_prev)
        def _():
            downs[r].start()

        rows(out_next, 2 * BB_DEV + r)

        @pl.when(has_next)
        def _():
            ups[r].start()

    def place(r, j):
        return slice(r * BLK, (r + 1) * BLK), slice(j * BLK, (j + 1) * BLK)

    for r in range(BB_DEV):
        own_row = row(BB_DEV + r)
        for j in range(5 * BB_DEV):
            if BB_DEV <= j < 4 * BB_DEV:
                band[place(r, j)] = put(screen, j - BB_DEV, own_row)
            else:
                band[place(r, j)] = zero

    @pl.when(has_prev)
    def _():
        for cut in range(CUTS):
            occ_down[cut].wait_send()
        id_down.wait_send()
        id_up.wait_recv()
        unit_down.wait_send()
        unit_up.wait_recv()

    @pl.when(has_next)
    def _():
        for cut in range(CUTS):
            occ_up[cut].wait_send()
        id_up.wait_send()
        id_down.wait_recv()
        unit_up.wait_send()
        unit_down.wait_recv()

    for r in range(BB_DEV):

        @pl.when(has_prev)
        def _():
            ups[r].wait_recv()
            came = [decode(in_prev[r, t], unit_prev) for t in range(NSB)]
            for j in range(3 * BB_DEV):
                band[place(r, j)] += put(ids_prev, j, came)

        @pl.when(has_next)
        def _():
            downs[r].wait_recv()
            came = [decode(in_next[r, t], unit_next) for t in range(NSB)]
            for j in range(3 * BB_DEV):
                band[place(r, j + 2 * BB_DEV)] += put(ids_next, j, came)

    @pl.when(has_prev)
    def _():
        for r in range(BB_DEV):
            downs[r].wait_send()

    @pl.when(has_next)
    def _():
        for r in range(BB_DEV):
            ups[r].wait_send()


def solution(mesh):
    count = mesh.shape["aux"]

    def shards(integrals, coeff, screen, occ_ids):
        aux_rows = integrals.shape[0]
        ints = jnp.transpose(integrals, (0, 1, 3, 2, 4))
        vmem = pl.BlockSpec(memory_space=pltpu.VMEM)
        nocc = OCCB * BLK
        dma = pltpu.SemaphoreType.DMA
        return pl.pallas_call(
            lambda *refs: kernel(count, *refs),
            out_shape=jax.ShapeDtypeStruct((EDGE, 5 * EDGE), jnp.float32),
            in_specs=[pl.BlockSpec(memory_space=pltpu.HBM)] * 4,
            out_specs=vmem,
            scratch_shapes=[
                pltpu.VMEM(coeff.shape, coeff.dtype),
                pltpu.SMEM(screen.shape, screen.dtype),
                pltpu.SMEM(occ_ids.shape, occ_ids.dtype),
                pltpu.VMEM((aux_rows, NSB, NSB, BLK, BLK), jnp.bfloat16),
                pltpu.VMEM((CUTS, 3 * BB_DEV, BLK, PART * BLK), jnp.bfloat16),
                pltpu.VMEM((CUTS, NSB * BLK, PART * BLK), jnp.bfloat16),
                pltpu.VMEM((NSB * BLK, NSB * BLK), jnp.float32),
                pltpu.VMEM((NSB * NSB, BLK, BLK), jnp.float32),
                pltpu.VMEM((BB_DEV, NSB, BLK, BLK), jnp.bfloat16),
                pltpu.VMEM((BB_DEV, NSB, BLK, BLK), jnp.bfloat16),
                pltpu.VMEM((BB_DEV, NSB, BLK, BLK), jnp.bfloat16),
                pltpu.VMEM((BB_DEV, NSB, BLK, BLK), jnp.bfloat16),
                pltpu.SMEM((1, NSB), jnp.int32),
                pltpu.SMEM((1, NSB), jnp.int32),
                dma((aux_rows // STEP,)),
                dma((2 * CUTS,)),
                dma((2 * CUTS,)),
                dma((2,)),
                dma((2,)),
                dma((4,)),
                dma((4,)),
                dma((3,)),
                pltpu.VMEM((8, BLK), jnp.float32),
                pltpu.VMEM((8, BLK), jnp.float32),
                pltpu.VMEM((8, BLK), jnp.float32),
                dma((2,)),
                dma((2,)),
            ],
            compiler_params=pltpu.CompilerParams(
                collective_id=0, has_side_effects=True, vmem_limit_bytes=56 * MIB),
            cost_estimate=pl.CostEstimate(
                flops=4 * aux_rows * NSB * BLK * NSB * BLK * nocc, transcendentals=0,
                bytes_accessed=aux_rows * (NSB * BLK) ** 2 * 2),
        )(ints, coeff, screen, occ_ids)

    return jax.shard_map(
        shards,
        mesh=mesh,
        in_specs=(
            P(("groups", "aux"), None, None, None, None),
            P(("groups", "aux"), None),
            P(("groups", "aux"), None),
            P("groups"),
        ),
        out_specs=P(("groups", "aux"), None),
        check_vma=False,
    )
```
